512 devices in a mesh: dp: 64 (over z, x), tensor: 8 (over y, core).
Axes of the slice: x: 4, y: 4, z: 16, core: 2. Of those that a mesh axis runs over, the one named last changes fastest.
Arguments:
- grad_query: bfloat16 [64, 1024, 2048], P('dp', None, 'tensor'), may hold values from -6 to 6
- error_query: bfloat16 [64, 1024, 2048], P('dp', None, 'tensor'), may hold values from -4 to 4
- basis_query: float32 [2048, 32], P('tensor'), may hold values from -6 to 6
- grad_output: bfloat16 [64, 2048, 1024], P('dp', 'tensor'), may hold values from -6 to 6
- error_output: bfloat16 [64, 2048, 1024], P('dp', 'tensor'), may hold values from -4 to 4
- basis_output: float32 [1024, 32], replicated, may hold values from -6 to 6
Outputs:
- reduced_query: bfloat16 [1024, 2048], P(None, 'tensor')
- reduced_output: bfloat16 [2048, 1024], P('tensor')
- error_query_next: bfloat16 [64, 1024, 2048], P('dp', None, 'tensor')
- error_output_next: bfloat16 [64, 2048, 1024], P('dp', 'tensor')
- basis_query_next: float32 [2048, 32], P('tensor')
- basis_output_next: float32 [1024, 32], replicated
The draws below stay inside these ranges and needn't reach their ends.
All inputs are finite; a program needn't handle non-finite values.
Results may differ from the reference program's by a relative error of at most 0.001.
Values sent between devices are 32-bit elements; how exact they have to be, the bound alone decides.
A program may use at most 64 MiB of HBM per device.

```python
import jax
import jax.numpy as jnp
from jax import lax

D = 2048
DWIN = 1024
R = 32
N_DP = 64


def shard_levels(rng, shape, cuts, least, top_value):
    level = 1.0
    for position, blocks in cuts:
        draws = jax.random.uniform(jax.random.fold_in(jax.random.fold_in(rng, 6), position), (blocks,), jnp.float32, least / len(cuts), top_value / len(cuts))
        level = level * jnp.repeat(jnp.exp(draws), shape[position] // blocks).reshape((-1,) + (1,) * (len(shape) - 1 - position))
    return level


def bell_draw(own_key, dims, deviation, bound, cuts=(), held_as=jnp.bfloat16):
    array = jax.random.normal(own_key, dims, jnp.float32) * deviation
    if len(cuts) > 0:
        array = shard_levels(own_key, dims, cuts, -0.22, 0.18) * array
    return jnp.clip(array, min=-bound, max=bound).astype(held_as)


def setup_inputs(seed: int = 0) -> dict:
    streams_of = jax.random.split(jax.random.key(seed), 7)
    return {
        "grad_query": bell_draw(streams_of[0], (N_DP, DWIN, D), 1.0, 6.0, ((0, 64), (2, 8))),
        "error_query": bell_draw(streams_of[1], (N_DP, DWIN, D), 0.5, 4.0, ((0, 64), (2, 8))),
        "basis_query": bell_draw(streams_of[2], (D, R), 1.0, 6.0, ((0, 8),), jnp.float32),
        "grad_output": bell_draw(streams_of[3], (N_DP, D, DWIN), 1.0, 6.0, ((0, 64), (1, 8))),
        "error_output": bell_draw(streams_of[4], (N_DP, D, DWIN), 0.5, 4.0, ((0, 64), (1, 8))),
        "basis_output": bell_draw(streams_of[5], (DWIN, R), 1.0, 6.0, (), jnp.float32),
    }


def orthonormal(factor):
    gram_matrix = jnp.dot(factor.T.astype(jnp.float32), factor.astype(jnp.float32), precision=lax.Precision.HIGHEST, preferred_element_type=jnp.float32)
    lower_factor = jnp.linalg.cholesky(gram_matrix)
    return lax.linalg.triangular_solve(lower_factor, factor, left_side=False, lower=True, transpose_a=True)

def compress(grads, errors, basis):
    rows = grads.shape[1]
    cols = grads.shape[2]

    def left_step(total, pieces):
        merged = pieces[0].astype(jnp.float32) + pieces[1].astype(jnp.float32)
        return (total + jnp.dot(merged.astype(jnp.float32), basis.astype(jnp.float32), precision=lax.Precision.HIGHEST, preferred_element_type=jnp.float32), None)
    left_total, _ = lax.scan(left_step, jnp.zeros((rows, R), jnp.float32), (grads, errors))
    unit_factor = orthonormal(left_total)

    def right_step(total, pieces):
        merged = pieces[0].astype(jnp.float32) + pieces[1].astype(jnp.float32)
        return (total + jnp.dot(merged.T.astype(jnp.float32), unit_factor.astype(jnp.float32), precision=lax.Precision.HIGHEST, preferred_element_type=jnp.float32), None)
    right_total, _ = lax.scan(right_step, jnp.zeros((cols, R), jnp.float32), (grads, errors))
    approx = jnp.dot(unit_factor.astype(jnp.float32), right_total.T.astype(jnp.float32), precision=lax.Precision.HIGHEST, preferred_element_type=jnp.float32)

    def new_error(pieces):
        merged = pieces[0].astype(jnp.float32) + pieces[1].astype(jnp.float32)
        return (merged - approx / N_DP).astype(jnp.bfloat16)
    errors_next = lax.map(new_error, (grads, errors))
    return (approx.astype(jnp.bfloat16), errors_next, right_total)

def reference(grad_query, error_query, basis_query, grad_output, error_output, basis_output):
    reduced_query, error_query_next, basis_query_next = compress(grad_query, error_query, basis_query)
    reduced_output, error_output_next, basis_output_next = compress(grad_output, error_output, basis_output)
    return (reduced_query, reduced_output, error_query_next, error_output_next, basis_query_next, basis_output_next)
```

```python
import functools

import jax
import jax.numpy as jnp
from jax import lax
from jax.experimental import pallas as pl
from jax.experimental.pallas import tpu as pltpu
from jax.sharding import PartitionSpec as P

MESH = pl.DeviceIdType.MESH
F32 = jnp.float32
BF16 = jnp.bfloat16
R = 32
LANES = 128


def split3(a):
    high = a.astype(BF16)
    rest = a - high.astype(F32)
    middle = rest.astype(BF16)
    low = (rest - middle.astype(F32)).astype(BF16)
    return jnp.concatenate([high, middle, low], axis=0)


def fold3(p):
    return (p[2 * R :] + p[R : 2 * R]) + p[:R]


def rows_by_rows(a, m):
    return lax.dot_general(a, m, (((1,), (1,)), ((), ())), preferred_element_type=F32)


def rows_by_columns(a, m):
    return lax.dot_general(a, m, (((1,), (0,)), ((), ())), preferred_element_type=F32)


def exact(a, b, dims):
    return lax.dot_general(
        a, b, (dims, ((), ())), precision=lax.Precision.HIGHEST, preferred_element_type=F32
    )


def eliminate(work, first, last):
    row = lax.broadcasted_iota(jnp.int32, work.shape, 0)
    for j in range(first, last):
        pivot = work[j : j + 1, j : j + 1]
        inverse = lax.rsqrt(pivot)
        inverse = inverse * (1.5 - 0.5 * (pivot * inverse) * inverse)
        scaled = work[j : j + 1, :] * inverse
        column = work[:, j : j + 1] * inverse
        work = jnp.where(row > j, work - column * scaled, jnp.where(row == j, scaled, work))
    return work


def augmented(gram):
    rows = lax.broadcasted_iota(jnp.int32, (R, R), 0)
    columns = lax.broadcasted_iota(jnp.int32, (R, R), 1)
    eye = jnp.where(rows == columns, 1.0, 0.0).astype(F32)
    return jnp.concatenate([gram, eye], axis=1)


def exchange(
    nt, nx, na, nb,
    gq_hbm, eq_hbm, bq_hbm, go_hbm, eo_hbm, bo_hbm,
    uq_out, rq_out, uo_out, ro_out,
    gq, eq, bq, go, eo, bo, load_sem,
    sq, so, rq, ro, za, zb, agq, ago, gram_all,
    send_sem, recv_sem,
):
    dp = lax.axis_index("dp")
    t = lax.axis_index("tensor")
    z = dp // nx
    x = lax.rem(dp, nx)
    b = z // na
    a = lax.rem(z, na)

    def at(x_, a_, b_, t_):
        return ((b_ * na + a_) * nx + x_, t_)

    def turn(i, d, n):
        return lax.rem(i + d, n)

    plane = [(dt, dx) for dx in range(nx) for dt in range(nt) if dt or dx]

    barrier = pltpu.get_barrier_semaphore()
    for dt, dx in plane:
        pl.semaphore_signal(
            barrier, inc=1, device_id=at(turn(x, dx, nx), a, b, turn(t, dt, nt)), device_id_type=MESH
        )
    for d in range(1, na):
        pl.semaphore_signal(barrier, inc=1, device_id=at(x, turn(a, d, na), b, t), device_id_type=MESH)
    for d in range(1, nb):
        pl.semaphore_signal(barrier, inc=1, device_id=at(x, a, turn(b, d, nb), t), device_id_type=MESH)

    loads = []
    for i, (source, target) in enumerate(
        ((bq_hbm, bq), (gq_hbm, gq), (eq_hbm, eq), (bo_hbm, bo), (go_hbm, go), (eo_hbm, eo))
    ):
        copy = pltpu.make_async_copy(source, target, load_sem.at[i])
        copy.start()
        loads.append(copy)

    def remote(source, target, k, device):
        pltpu.make_async_remote_copy(
            src_ref=source, dst_ref=target, send_sem=send_sem.at[k], recv_sem=recv_sem.at[k],
            device_id=device, device_id_type=MESH,
        ).start()

    def arrived(ref, k):
        pltpu.make_async_copy(ref, ref, recv_sem.at[k]).wait()

    def sent(ref, k):
        pltpu.make_async_copy(ref, ref, send_sem.at[k]).wait()

    def scatter(p, wide, narrow):
        k = 8 * p
        part = R // nx
        for i in range(nt):
            for j in range(nx):
                sq[p, i, j] = wide[j * part : (j + 1) * part, i * LANES : (i + 1) * LANES]
        for j in range(nx):
            so[p, j] = narrow[j * part : (j + 1) * part]
        for dx in range(1, nx):
            there = turn(x, dx, nx)
            remote(so.at[p, there], ro.at[p, dx - 1], k + 1, at(there, a, b, t))
        for i, (dt, dx) in enumerate(plane):
            tt, xx = turn(t, dt, nt), turn(x, dx, nx)
            remote(sq.at[p, tt, xx], rq.at[p, i], k, at(xx, a, b, tt))

    def gathered_sum(p):
        k = 8 * p
        arrived(ro.at[p], k + 1)
        narrow = so[p, x]
        for d in range(nx - 1):
            narrow = narrow + ro[p, d]
        arrived(rq.at[p], k)
        terms = [sq[p, t, x]] + [rq[p, i] for i in range(len(plane))]
        while len(terms) > 1:
            terms = [sum(terms[i : i + 2][1:], terms[i]) for i in range(0, len(terms), 2)]
        za[p, a, :, :LANES] = terms[0]
        za[p, a, :, LANES:] = narrow
        for d in range(1, na):
            remote(za.at[p, a], za.at[p, a], k + 2, at(x, turn(a, d, na), b, t))

    def along_a(p):
        k = 8 * p
        arrived(za.at[p, pl.ds(0, na - 1)], k + 2)
        total = za[p, 0]
        for i in range(1, na):
            total = total + za[p, i]
        zb[p, b] = total
        for d in range(1, nb):
            remote(zb.at[p, b], zb.at[p, b], k + 3, at(x, a, turn(b, d, nb), t))

    def along_b(p):
        k = 8 * p
        arrived(zb.at[p, pl.ds(0, nb - 1)], k + 3)
        total = zb[p, 0]
        for i in range(1, nb):
            total = total + zb[p, i]
        here = t * nx + x
        agq[p, here] = total[:, :LANES]
        ago[p, x] = total[:, LANES:]
        for dx in range(1, nx):
            remote(ago.at[p, x], ago.at[p, x], k + 5, at(turn(x, dx, nx), a, b, t))
        for dt, dx in plane:
            remote(agq.at[p, here], agq.at[p, here], k + 4, at(turn(x, dx, nx), a, b, turn(t, dt, nt)))

    def narrow_result(p):
        arrived(ago.at[p, pl.ds(0, nx - 1)], 8 * p + 5)
        return jnp.concatenate([ago[p, j] for j in range(nx)], axis=0)

    def wide_result(p):
        arrived(agq.at[p, pl.ds(0, nt * nx - 1)], 8 * p + 4)
        return jnp.concatenate(
            [jnp.concatenate([agq[p, i * nx + j] for j in range(nx)], axis=0) for i in range(nt)], axis=1
        )

    for i in range(3):
        loads[i].wait()
    terms = split3(bq[...].T)
    wide = fold3(rows_by_rows(terms, gq[...]) + rows_by_rows(terms, eq[...]))
    for i in range(3, 6):
        loads[i].wait()
    terms = split3(bo[...].T)
    narrow = fold3(rows_by_rows(terms, go[...]) + rows_by_rows(terms, eo[...]))
    pl.semaphore_wait(barrier, len(plane) + na - 1 + nb - 1)
    scatter(0, wide, narrow)
    gathered_sum(0)
    along_a(0)
    along_b(0)
    left_output = narrow_result(0)
    terms = split3(left_output)
    wide = fold3(rows_by_columns(terms, go[...]) + rows_by_columns(terms, eo[...]))
    left_query = wide_result(0)
    terms = split3(left_query)
    narrow = fold3(rows_by_columns(terms, gq[...]) + rows_by_columns(terms, eq[...]))

    scatter(1, wide, narrow)
    gram = exact(left_output, left_output, ((1,), (1,)))
    gram_all[t] = jnp.concatenate([gram, jnp.zeros((R, LANES - R), F32)], axis=1)
    for d in range(1, nt):
        remote(gram_all.at[t], gram_all.at[t], 6, at(x, a, b, turn(t, d, nt)))
    query_work = augmented(exact(left_query, left_query, ((1,), (1,))))
    gathered_sum(1)
    arrived(gram_all.at[pl.ds(0, nt - 1)], 6)
    gram = gram_all[0]
    for i in range(1, nt):
        gram = gram + gram_all[i]
    output_work = augmented(gram[:, :R])
    query_work = eliminate(query_work, 0, R // 2)
    output_work = eliminate(output_work, 0, R // 2)
    along_a(1)
    query_work = eliminate(query_work, R // 2, R)
    output_work = eliminate(output_work, R // 2, R)
    query_inverse = query_work[:, R : 2 * R]
    output_inverse = output_work[:, R : 2 * R]
    along_b(1)
    uq_out[...] = exact(query_inverse, left_query, ((1,), (0,)))
    uo_out[...] = exact(output_inverse, left_output, ((1,), (0,)))
    rq_out[...] = exact(query_inverse, narrow_result(1), ((1,), (0,)))
    ro_out[...] = exact(output_inverse, wide_result(1), ((1,), (0,)))

    for p in range(2):
        k = 8 * p
        sent(rq.at[p], k)
        sent(ro.at[p], k + 1)
        sent(za.at[p, pl.ds(0, na - 1)], k + 2)
        sent(zb.at[p, pl.ds(0, nb - 1)], k + 3)
        sent(agq.at[p, pl.ds(0, nt * nx - 1)], k + 4)
        sent(ago.at[p, pl.ds(0, nx - 1)], k + 5)
    sent(gram_all.at[pl.ds(0, nt - 1)], 6)


def stacked(left, right):
    left_high = left.astype(BF16)
    left_low = (left - left_high.astype(F32)).astype(BF16)
    right_high = right.astype(BF16)
    right_low = (right - right_high.astype(F32)).astype(BF16)
    return lax.dot_general(
        jnp.concatenate([left_high, left_low, left_high], axis=0),
        jnp.concatenate([right_high, right_high, right_low], axis=0),
        (((0,), (0,)), ((), ())),
        preferred_element_type=F32,
    )


def finish(
    replicas, uq, rq, uo, ro, gq, eq, go, eo,
    reduced_query, reduced_output, error_query, error_output, right_query, right_output,
):
    scale = 1.0 / replicas
    approx = stacked(uq[...], rq[...])
    reduced_query[...] = approx.astype(BF16)
    error_query[...] = (gq[...].astype(F32) + eq[...].astype(F32) - approx * scale).astype(BF16)
    approx = stacked(uo[...], ro[...])
    reduced_output[...] = approx.astype(BF16)
    error_output[...] = (go[...].astype(F32) + eo[...].astype(F32) - approx * scale).astype(BF16)
    right_query[...] = rq[...].T
    right_output[...] = ro[...].T


def local(sizes, grad_query, error_query, basis_query, grad_output, error_output, basis_output):
    nt, nx, na, nb = sizes
    gq, eq, go, eo = grad_query[0], error_query[0], grad_output[0], error_output[0]
    rows, columns = gq.shape
    hidden, features = go.shape
    part = R // nx
    any_space = pl.BlockSpec(memory_space=pl.ANY)
    vmem = pl.BlockSpec(memory_space=pltpu.VMEM)
    shape = jax.ShapeDtypeStruct
    uq, rq, uo, ro = pl.pallas_call(
        functools.partial(exchange, nt, nx, na, nb),
        out_shape=(
            shape((R, rows), F32), shape((R, columns), F32), shape((R, hidden), F32), shape((R, features), F32),
        ),
        in_specs=[any_space] * 6,
        out_specs=(vmem,) * 4,
        scratch_shapes=[
            pltpu.VMEM((rows, columns), BF16),
            pltpu.VMEM((rows, columns), BF16),
            pltpu.VMEM((columns, R), F32),
            pltpu.VMEM((hidden, features), BF16),
            pltpu.VMEM((hidden, features), BF16),
            pltpu.VMEM((features, R), F32),
            pltpu.SemaphoreType.DMA((6,)),
            pltpu.VMEM((2, nt, nx, part, LANES), F32),
            pltpu.VMEM((2, nx, part, hidden), F32),
            pltpu.VMEM((2, nt * nx - 1, part, LANES), F32),
            pltpu.VMEM((2, nx - 1, part, hidden), F32),
            pltpu.VMEM((2, na, part, LANES + hidden), F32),
            pltpu.VMEM((2, nb, part, LANES + hidden), F32),
            pltpu.VMEM((2, nt * nx, part, LANES), F32),
            pltpu.VMEM((2, nx, part, hidden), F32),
            pltpu.VMEM((nt, R, LANES), F32),
            pltpu.SemaphoreType.DMA((16,)),
            pltpu.SemaphoreType.DMA((16,)),
        ],
        compiler_params=pltpu.CompilerParams(
            collective_id=0, has_side_effects=True, vmem_limit_bytes=32 * 1024 * 1024
        ),
    )(gq, eq, basis_query, go, eo, basis_output)
    outs = pl.pallas_call(
        functools.partial(finish, nx * na * nb),
        out_shape=(
            shape((rows, columns), BF16), shape((hidden, features), BF16),
            shape((rows, columns), BF16), shape((hidden, features), BF16),
            shape((columns, R), F32), shape((features, R), F32),
        ),
        in_specs=[vmem] * 8,
        out_specs=(vmem,) * 6,
        compiler_params=pltpu.CompilerParams(vmem_limit_bytes=32 * 1024 * 1024),
    )(uq, rq, uo, ro, gq, eq, go, eo)
    return outs[0], outs[1], outs[2][None], outs[3][None], outs[4], outs[5]


def solution(mesh):
    nt, n = mesh.shape["tensor"], mesh.shape["dp"]
    nx = 4 if n >= 64 else 2
    na = 4 if n >= 64 else 2
    nb = n // (nx * na)
    return jax.shard_map(
        functools.partial(local, (nt, nx, na, nb)),
        mesh=mesh,
        in_specs=(
            P("dp", None, "tensor"),
            P("dp", None, "tensor"),
            P("tensor", None),
            P("dp", "tensor", None),
            P("dp", "tensor", None),
            P(),
        ),
        out_specs=(
            P(None, "tensor"),
            P("tensor", None),
            P("dp", None, "tensor"),
            P("dp", "tensor", None),
            P("tensor", None),
            P(),
        ),
        check_vma=False,
    )
```

```python
import functools

import jax
import jax.numpy as jnp
from jax import lax
from jax.experimental import pallas as pl
from jax.experimental.pallas import tpu as pltpu
from jax.sharding import PartitionSpec as P

MESH = pl.DeviceIdType.MESH
F32 = jnp.float32
BF16 = jnp.bfloat16
R = 32
LANES = 128


def split3(a):
    high = a.astype(BF16)
    rest = a - high.astype(F32)
    middle = rest.astype(BF16)
    low = (rest - middle.astype(F32)).astype(BF16)
    return jnp.concatenate([high, middle, low], axis=0)


def fold3(p):
    return (p[2 * R :] + p[R : 2 * R]) + p[:R]


def rows_by_rows(a, m):
    return lax.dot_general(a, m, (((1,), (1,)), ((), ())), preferred_element_type=F32)


def rows_by_columns(a, m):
    return lax.dot_general(a, m, (((1,), (0,)), ((), ())), preferred_element_type=F32)


def exact(a, b, dims):
    return lax.dot_general(
        a, b, (dims, ((), ())), precision=lax.Precision.HIGHEST, preferred_element_type=F32
    )


def eliminate(work, first, last):
    row = lax.broadcasted_iota(jnp.int32, work.shape, 0)
    for j in range(first, last):
        pivot = work[j : j + 1, j : j + 1]
        inverse = lax.rsqrt(pivot)
        inverse = inverse * (1.5 - 0.5 * (pivot * inverse) * inverse)
        scaled = work[j : j + 1, :] * inverse
        column = work[:, j : j + 1] * inverse
        work = jnp.where(row > j, work - column * scaled, jnp.where(row == j, scaled, work))
    return work


def augmented(gram):
    rows = lax.broadcasted_iota(jnp.int32, (R, R), 0)
    columns = lax.broadcasted_iota(jnp.int32, (R, R), 1)
    eye = jnp.where(rows == columns, 1.0, 0.0).astype(F32)
    return jnp.concatenate([gram, eye], axis=1)


def exchange(
    ny, nc, nx, na, nb,
    gq_hbm, eq_hbm, bq_hbm, go_hbm, eo_hbm, bo_hbm,
    uq_out, rq_out, uo_out, ro_out,
    gq, eq, bq, go, eo, bo, load_sem,
    wide_here, wide_in, wide_z, wide_all,
    thin_here, thin_in, thin_a, thin_b, thin_all,
    gram_all, send_sem, recv_sem,
):
    nt, nz = ny * nc, na * nb
    part = R // nx
    dp = lax.axis_index("dp")
    t = lax.axis_index("tensor")
    z = dp // nx
    x = lax.rem(dp, nx)
    b = z // na
    a = lax.rem(z, na)
    y = t // nc
    c = lax.rem(t, nc)

    def hops(d, n):
        return min(d, n - d)

    plane = sorted(
        ((dy, dc, dx) for dx in range(nx) for dy in range(ny) for dc in range(nc) if dx or dy or dc),
        key=lambda d: -hops(d[0], ny) - hops(d[2], nx),
    )
    along_z = sorted(range(1, nz), key=lambda d: -hops(d, nz))
    along_x = sorted(range(1, nx), key=lambda d: -hops(d, nx))

    def turned_t(dy, dc):
        return lax.rem(y + dy, ny) * nc + lax.rem(c + dc, nc)

    def turned_x(dx):
        return lax.rem(x + dx, nx)

    def in_plane(t_, x_):
        return (z * nx + x_, t_)

    def at_z(z_):
        return (z_ * nx + x, t)

    def signal(device):
        pl.semaphore_signal(barrier, inc=1, device_id=device, device_id_type=MESH)

    barrier = pltpu.get_barrier_semaphore()
    for d in along_z:
        signal(at_z(lax.rem(z + d, nz)))
    for dy, dc, dx in plane:
        signal(in_plane(turned_t(dy, dc), turned_x(dx)))

    loads = []
    for i, (source, target) in enumerate(
        ((bo_hbm, bo), (go_hbm, go), (eo_hbm, eo), (bq_hbm, bq), (gq_hbm, gq), (eq_hbm, eq))
    ):
        copy = pltpu.make_async_copy(source, target, load_sem.at[i])
        copy.start()
        loads.append(copy)

    def remote(source, target, k, device):
        pltpu.make_async_remote_copy(
            src_ref=source, dst_ref=target, send_sem=send_sem.at[k], recv_sem=recv_sem.at[k],
            device_id=device, device_id_type=MESH,
        ).start()

    def arrived(ref, k):
        pltpu.make_async_copy(ref, ref, recv_sem.at[k]).wait()

    def sent(ref, k):
        pltpu.make_async_copy(ref, ref, send_sem.at[k]).wait()

    def total(terms):
        while len(terms) > 1:
            pairs = [terms[i] + terms[i + 1] for i in range(0, len(terms) - 1, 2)]
            terms = pairs + terms[len(pairs) * 2 :]
        return terms[0]

    def wide_scatter(p, value):
        for i in range(nt):
            for j in range(nx):
                wide_here[p, i, j] = value[j * part : (j + 1) * part, i * LANES : (i + 1) * LANES]
        for i, (dy, dc, dx) in enumerate(plane):
            t_, x_ = turned_t(dy, dc), turned_x(dx)
            remote(wide_here.at[p, t_, x_], wide_in.at[p, i], 8 * p, in_plane(t_, x_))

    def wide_exchange(p):
        arrived(wide_in.at[p], 8 * p)
        wide_z[p, z] = total([wide_here[p, t, x]] + [wide_in[p, i] for i in range(len(plane))])
        for d in along_z:
            remote(wide_z.at[p, z], wide_z.at[p, z], 8 * p + 1, at_z(lax.rem(z + d, nz)))

    def wide_gather(p):
        arrived(wide_z.at[p, pl.ds(0, nz - 1)], 8 * p + 1)
        here = t * nx + x
        wide_all[p, here] = total([wide_z[p, i] for i in range(nz)])
        for dy, dc, dx in plane:
            remote(
                wide_all.at[p, here], wide_all.at[p, here], 8 * p + 2, in_plane(turned_t(dy, dc), turned_x(dx))
            )

    def wide_result(p):
        arrived(wide_all.at[p, pl.ds(0, nt * nx - 1)], 8 * p + 2)
        return jnp.concatenate(
            [jnp.concatenate([wide_all[p, i * nx + j] for j in range(nx)], axis=0) for i in range(nt)], axis=1
        )

    def thin_scatter(p, value):
        for j in range(nx):
            thin_here[p, j] = value[j * part : (j + 1) * part]
        for i, dx in enumerate(along_x):
            x_ = turned_x(dx)
            remote(thin_here.at[p, x_], thin_in.at[p, i], 8 * p + 3, in_plane(t, x_))

    def thin_near(p):
        arrived(thin_in.at[p], 8 * p + 3)
        thin_a[p, a] = total([thin_here[p, x]] + [thin_in[p, i] for i in range(nx - 1)])
        for d in range(1, na):
            remote(thin_a.at[p, a], thin_a.at[p, a], 8 * p + 4, at_z(b * na + lax.rem(a + d, na)))

    def thin_far(p):
        arrived(thin_a.at[p, pl.ds(0, na - 1)], 8 * p + 4)
        thin_b[p, b] = total([thin_a[p, i] for i in range(na)])
        for d in range(1, nb):
            remote(thin_b.at[p, b], thin_b.at[p, b], 8 * p + 5, at_z(lax.rem(b + d, nb) * na + a))

    def thin_gather(p):
        arrived(thin_b.at[p, pl.ds(0, nb - 1)], 8 * p + 5)
        thin_all[p, x] = total([thin_b[p, i] for i in range(nb)])
        for dx in along_x:
            remote(thin_all.at[p, x], thin_all.at[p, x], 8 * p + 6, in_plane(t, turned_x(dx)))

    def thin_result(p):
        arrived(thin_all.at[p, pl.ds(0, nx - 1)], 8 * p + 6)
        return jnp.concatenate([thin_all[p, j] for j in range(nx)], axis=0)

    for i in range(3):
        loads[i].wait()
    terms = split3(bo[...])
    value = fold3(rows_by_rows(terms, go[...]) + rows_by_rows(terms, eo[...]))
    pl.semaphore_wait(barrier, len(plane) + len(along_z))
    thin_scatter(0, value)
    for i in range(3, 6):
        loads[i].wait()
    terms = split3(bq[...])
    value = fold3(rows_by_rows(terms, gq[...]) + rows_by_rows(terms, eq[...]))
    wide_scatter(0, value)
    thin_near(0)
    wide_exchange(0)
    thin_far(0)
    thin_gather(0)
    wide_gather(0)

    left_output = thin_result(0)
    terms = split3(left_output)
    value = fold3(rows_by_columns(terms, go[...]) + rows_by_columns(terms, eo[...]))
    wide_scatter(1, value)
    gram = exact(left_output, left_output, ((1,), (1,)))
    gram_all[t] = jnp.concatenate([gram[i : i + 8] for i in range(0, R, 8)], axis=1)
    for dy, dc, dx in plane:
        if dx == 0:
            remote(gram_all.at[t], gram_all.at[t], 7, in_plane(turned_t(dy, dc), x))
    left_query = wide_result(0)
    terms = split3(left_query)
    value = fold3(rows_by_columns(terms, gq[...]) + rows_by_columns(terms, eq[...]))
    thin_scatter(1, value)
    query_work = augmented(exact(left_query, left_query, ((1,), (1,))))
    wide_exchange(1)
    thin_near(1)
    arrived(gram_all.at[pl.ds(0, nt - 1)], 7)
    gram = total([gram_all[i] for i in range(nt)])
    gram = jnp.concatenate([gram[:, i : i + R] for i in range(0, 4 * R, R)], axis=0)
    output_work = augmented(gram)
    query_work = eliminate(query_work, 0, R // 2)
    output_work = eliminate(output_work, 0, R // 2)
    thin_far(1)
    query_work = eliminate(query_work, R // 2, R)
    output_work = eliminate(output_work, R // 2, R)
    query_inverse = query_work[:, R : 2 * R]
    output_inverse = output_work[:, R : 2 * R]
    uq_out[...] = exact(query_inverse, left_query, ((1,), (0,)))
    uo_out[...] = exact(output_inverse, left_output, ((1,), (0,)))
    wide_gather(1)
    thin_gather(1)
    ro_out[...] = exact(output_inverse, wide_result(1), ((1,), (0,)))
    rq_out[...] = exact(query_inverse, thin_result(1), ((1,), (0,)))

    for p in range(2):
        k = 8 * p
        sent(wide_in.at[p], k)
        sent(wide_z.at[p, pl.ds(0, nz - 1)], k + 1)
        sent(wide_all.at[p, pl.ds(0, nt * nx - 1)], k + 2)
        sent(thin_in.at[p], k + 3)
        sent(thin_a.at[p, pl.ds(0, na - 1)], k + 4)
        sent(thin_b.at[p, pl.ds(0, nb - 1)], k + 5)
        sent(thin_all.at[p, pl.ds(0, nx - 1)], k + 6)
    sent(gram_all.at[pl.ds(0, nt - 1)], 7)


def stacked(left, right):
    left_high = left.astype(BF16)
    left_low = (left - left_high.astype(F32)).astype(BF16)
    right_high = right.astype(BF16)
    right_low = (right - right_high.astype(F32)).astype(BF16)
    return lax.dot_general(
        jnp.concatenate([left_high, left_low, left_high], axis=0),
        jnp.concatenate([right_high, right_high, right_low], axis=0),
        (((0,), (0,)), ((), ())),
        preferred_element_type=F32,
    )


def finish(
    replicas, uq, rq, uo, ro, gq, eq, go, eo,
    reduced_query, reduced_output, error_query, error_output, right_query, right_output,
):
    scale = 1.0 / replicas
    approx = stacked(uq[...], rq[...])
    reduced_query[...] = approx.astype(BF16)
    error_query[...] = (gq[...].astype(F32) + eq[...].astype(F32) - approx * scale).astype(BF16)
    approx = stacked(uo[...], ro[...])
    reduced_output[...] = approx.astype(BF16)
    error_output[...] = (go[...].astype(F32) + eo[...].astype(F32) - approx * scale).astype(BF16)
    right_query[...] = rq[...]
    right_output[...] = ro[...]


def local(sizes, grad_query, error_query, basis_query, grad_output, error_output, basis_output):
    ny, nc, nx, na, nb = sizes
    nt = ny * nc
    gq, eq, go, eo = grad_query[0], error_query[0], grad_output[0], error_output[0]
    rows, columns = gq.shape
    hidden, features = go.shape
    part = R // nx
    hbm = pl.BlockSpec(memory_space=pltpu.HBM)
    vmem = pl.BlockSpec(memory_space=pltpu.VMEM)
    shape = jax.ShapeDtypeStruct
    uq, rq, uo, ro = pl.pallas_call(
        functools.partial(exchange, ny, nc, nx, na, nb),
        out_shape=(
            shape((R, rows), F32), shape((R, columns), F32), shape((R, hidden), F32), shape((R, features), F32),
        ),
        in_specs=[hbm] * 6,
        out_specs=(vmem,) * 4,
        scratch_shapes=[
            pltpu.VMEM((rows, columns), BF16),
            pltpu.VMEM((rows, columns), BF16),
            pltpu.VMEM((R, columns), F32),
            pltpu.VMEM((hidden, features), BF16),
            pltpu.VMEM((hidden, features), BF16),
            pltpu.VMEM((R, features), F32),
            pltpu.SemaphoreType.DMA((6,)),
            pltpu.VMEM((2, nt, nx, part, LANES), F32),
            pltpu.VMEM((2, nt * nx - 1, part, LANES), F32),
            pltpu.VMEM((2, na * nb, part, LANES), F32),
            pltpu.VMEM((2, nt * nx, part, LANES), F32),
            pltpu.VMEM((2, nx, part, hidden), F32),
            pltpu.VMEM((2, nx - 1, part, hidden), F32),
            pltpu.VMEM((2, na, part, hidden), F32),
            pltpu.VMEM((2, nb, part, hidden), F32),
            pltpu.VMEM((2, nx, part, hidden), F32),
            pltpu.VMEM((nt, 8, LANES), F32),
            pltpu.SemaphoreType.DMA((16,)),
            pltpu.SemaphoreType.DMA((16,)),
        ],
        compiler_params=pltpu.CompilerParams(
            collective_id=0, has_side_effects=True, vmem_limit_bytes=60 * 1024 * 1024
        ),
    )(gq, eq, basis_query.T, go, eo, basis_output.T)
    outs = pl.pallas_call(
        functools.partial(finish, nx * na * nb),
        out_shape=(
            shape((rows, columns), BF16), shape((hidden, features), BF16),
            shape((rows, columns), BF16), shape((hidden, features), BF16),
            shape((R, columns), F32), shape((R, features), F32),
        ),
        in_specs=[vmem] * 8,
        out_specs=(vmem,) * 6,
        compiler_params=pltpu.CompilerParams(vmem_limit_bytes=60 * 1024 * 1024),
    )(uq, rq, uo, ro, gq, eq, go, eo)
    return outs[0], outs[1], outs[2][None], outs[3][None], outs[4].T, outs[5].T


def solution(mesh):
    nt, n = mesh.shape["tensor"], mesh.shape["dp"]
    nx = 4 if n >= 64 else 2
    na = 4 if n >= 64 else 2
    nb = n // (nx * na)
    return jax.shard_map(
        functools.partial(local, (nt // 2, 2, nx, na, nb)),
        mesh=mesh,
        in_specs=(
            P("dp", None, "tensor"),
            P("dp", None, "tensor"),
            P("tensor", None),
            P("dp", "tensor", None),
            P("dp", "tensor", None),
            P(),
        ),
        out_specs=(
            P(None, "tensor"),
            P("tensor", None),
            P("dp", None, "tensor"),
            P("dp", "tensor", None),
            P("tensor", None),
            P(),
        ),
        check_vma=False,
    )
```

```python
import functools

import jax
import jax.numpy as jnp
from jax import lax
from jax.experimental import pallas as pl
from jax.experimental.pallas import tpu as pltpu
from jax.sharding import PartitionSpec as P

MESH = pl.DeviceIdType.MESH
F32 = jnp.float32
BF16 = jnp.bfloat16
R = 32
LANES = 128


def split3(a):
    high = a.astype(BF16)
    rest = a - high.astype(F32)
    middle = rest.astype(BF16)
    low = (rest - middle.astype(F32)).astype(BF16)
    return jnp.concatenate([high, middle, low], axis=0)


def fold3(p):
    return (p[2 * R :] + p[R : 2 * R]) + p[:R]


def rows_by_rows(a, m):
    return lax.dot_general(a, m, (((1,), (1,)), ((), ())), preferred_element_type=F32)


def rows_by_columns(a, m):
    return lax.dot_general(a, m, (((1,), (0,)), ((), ())), preferred_element_type=F32)


def exact(a, b, dims):
    return lax.dot_general(
        a, b, (dims, ((), ())), precision=lax.Precision.HIGHEST, preferred_element_type=F32
    )


def eliminate(work, first, last):
    row = lax.broadcasted_iota(jnp.int32, work.shape, 0)
    for j in range(first, last):
        pivot = work[j : j + 1, j : j + 1]
        inverse = lax.rsqrt(pivot)
        inverse = inverse * (1.5 - 0.5 * (pivot * inverse) * inverse)
        scaled = work[j : j + 1, :] * inverse
        column = work[:, j : j + 1] * inverse
        work = jnp.where(row > j, work - column * scaled, jnp.where(row == j, scaled, work))
    return work


def augmented(gram):
    rows = lax.broadcasted_iota(jnp.int32, (R, R), 0)
    columns = lax.broadcasted_iota(jnp.int32, (R, R), 1)
    eye = jnp.where(rows == columns, 1.0, 0.0).astype(F32)
    return jnp.concatenate([gram, eye], axis=1)


def exchange(
    ny, nc, nx, nz,
    gq_hbm, eq_hbm, bq_hbm, go_hbm, eo_hbm, bo_hbm,
    uq_out, rq_out, uo_out, ro_out,
    gq, eq, bq, go, eo, bo, load_sem,
    wide_here, wide_in, wide_z, wide_all,
    thin_here, thin_in, thin_z, thin_zll,
    gram_all, send_sem, recv_sem, relay_sem,
):
    nt = ny * nc
    part = R // nx
    dp = lax.axis_index("dp")
    t = lax.axis_index("tensor")
    z = dp // nx
    x = lax.rem(dp, nx)
    y = t // nc
    c = lax.rem(t, nc)

    def hops(d, n):
        return min(d, n - d)

    plane = sorted(
        ((dy, dc, dx) for dx in range(nx) for dy in range(ny) for dc in range(nc) if dx or dy or dc),
        key=lambda d: -hops(d[0], ny) - hops(d[2], nx),
    )
    along_z = sorted(range(1, nz), key=lambda d: -hops(d, nz))
    reach = nz // 4
    along_x = sorted(range(1, nx), key=lambda d: -hops(d, nx))

    def turned_t(dy, dc):
        return lax.rem(y + dy, ny) * nc + lax.rem(c + dc, nc)

    def turned_x(dx):
        return lax.rem(x + dx, nx)

    def in_plane(t_, x_):
        return (z * nx + x_, t_)

    def at_z(z_):
        return (z_ * nx + x, t)

    def signal(device):
        pl.semaphore_signal(barrier, inc=1, device_id=device, device_id_type=MESH)

    barrier = pltpu.get_barrier_semaphore()
    for d in along_z:
        if hops(d, nz) <= reach:
            signal(at_z(lax.rem(z + d, nz)))

    loads = []
    for i, (source, target) in enumerate(
        ((bo_hbm, bo), (go_hbm, go), (eo_hbm, eo), (bq_hbm, bq), (gq_hbm, gq), (eq_hbm, eq))
    ):
        copy = pltpu.make_async_copy(source, target, load_sem.at[i])
        copy.start()
        loads.append(copy)

    for dy, dc, dx in plane:
        signal(in_plane(turned_t(dy, dc), turned_x(dx)))

    def remote(source, target, k, device):
        pltpu.make_async_remote_copy(
            src_ref=source, dst_ref=target, send_sem=send_sem.at[k], recv_sem=recv_sem.at[k],
            device_id=device, device_id_type=MESH,
        ).start()

    def arrived(ref, k):
        pltpu.make_async_copy(ref, ref, recv_sem.at[k]).wait()

    def sent(ref, k):
        pltpu.make_async_copy(ref, ref, send_sem.at[k]).wait()

    def total(terms):
        while len(terms) > 1:
            pairs = [terms[i] + terms[i + 1] for i in range(0, len(terms) - 1, 2)]
            terms = pairs + terms[len(pairs) * 2 :]
        return terms[0]

    def wide_scatter(p, value):
        for i in range(nt):
            for j in range(nx):
                wide_here[p, i, j] = value[j * part : (j + 1) * part, i * LANES : (i + 1) * LANES]
        for i, (dy, dc, dx) in enumerate(plane):
            t_, x_ = turned_t(dy, dc), turned_x(dx)
            remote(wide_here.at[p, t_, x_], wide_in.at[p, i], 8 * p, in_plane(t_, x_))

    def wide_exchange(p):
        arrived(wide_in.at[p], 8 * p)
        wide_z[p, z] = total([wide_here[p, t, x]] + [wide_in[p, i] for i in range(len(plane))])
        for d in along_z:
            remote(wide_z.at[p, z], wide_z.at[p, z], 8 * p + 1, at_z(lax.rem(z + d, nz)))

    def wide_gather(p):
        arrived(wide_z.at[p, pl.ds(0, nz - 1)], 8 * p + 1)
        here = t * nx + x
        wide_all[p, here] = total([wide_z[p, i] for i in range(nz)])
        for dy, dc, dx in plane:
            remote(
                wide_all.at[p, here], wide_all.at[p, here], 8 * p + 2, in_plane(turned_t(dy, dc), turned_x(dx))
            )

    def wide_result(p):
        arrived(wide_all.at[p, pl.ds(0, nt * nx - 1)], 8 * p + 2)
        return jnp.concatenate(
            [jnp.concatenate([wide_all[p, i * nx + j] for j in range(nx)], axis=0) for i in range(nt)], axis=1
        )

    def thin_scatter(p, value):
        for j in range(nx):
            thin_here[p, j] = value[j * part : (j + 1) * part]
        for i, dx in enumerate(along_x):
            x_ = turned_x(dx)
            remote(thin_here.at[p, x_], thin_in.at[p, i], 8 * p + 3, in_plane(t, x_))

    def thin_exchange(p):
        arrived(thin_in.at[p], 8 * p + 3)
        thin_z[p, z] = total([thin_here[p, x]] + [thin_in[p, i] for i in range(nx - 1)])
        for d in along_z:
            remote(thin_z.at[p, z], thin_z.at[p, z], 8 * p + 4, at_z(lax.rem(z + d, nz)))

    def thin_gather(p):
        arrived(thin_z.at[p, pl.ds(0, nz - 1)], 8 * p + 4)
        thin_zll[p, x] = total([thin_z[p, i] for i in range(nz)])
        for dx in along_x:
            remote(thin_zll.at[p, x], thin_zll.at[p, x], 8 * p + 6, in_plane(t, turned_x(dx)))

    def thin_result(p):
        arrived(thin_zll.at[p, pl.ds(0, nx - 1)], 8 * p + 6)
        return jnp.concatenate([thin_zll[p, j] for j in range(nx)], axis=0)

    for i in range(3):
        loads[i].wait()
    terms = split3(bo[...])
    value = fold3(rows_by_rows(terms, go[...]) + rows_by_rows(terms, eo[...]))
    pl.semaphore_wait(barrier, len(plane) + 2 * reach)
    for d in (reach, nz - reach):
        pl.semaphore_signal(relay_sem, inc=1, device_id=at_z(lax.rem(z + d, nz)), device_id_type=MESH)
    thin_scatter(0, value)
    for i in range(3, 6):
        loads[i].wait()
    terms = split3(bq[...])
    value = fold3(rows_by_rows(terms, gq[...]) + rows_by_rows(terms, eq[...]))
    wide_scatter(0, value)
    pl.semaphore_wait(relay_sem, 2)
    thin_exchange(0)
    wide_exchange(0)
    thin_gather(0)
    wide_gather(0)

    left_output = thin_result(0)
    terms = split3(left_output)
    value = fold3(rows_by_columns(terms, go[...]) + rows_by_columns(terms, eo[...]))
    wide_scatter(1, value)
    left_query = wide_result(0)
    terms = split3(left_query)
    value = fold3(rows_by_columns(terms, gq[...]) + rows_by_columns(terms, eq[...]))
    thin_scatter(1, value)
    gram = exact(left_output, left_output, ((1,), (1,)))
    gram_all[t] = jnp.concatenate([gram[i : i + 8] for i in range(0, R, 8)], axis=1)
    for dy, dc, dx in plane:
        if dx == 0:
            remote(gram_all.at[t], gram_all.at[t], 7, in_plane(turned_t(dy, dc), x))
    query_work = augmented(exact(left_query, left_query, ((1,), (1,))))
    query_work = eliminate(query_work, 0, 12)
    wide_exchange(1)
    thin_exchange(1)
    query_work = eliminate(query_work, 12, R)
    arrived(gram_all.at[pl.ds(0, nt - 1)], 7)
    gram = total([gram_all[i] for i in range(nt)])
    gram = jnp.concatenate([gram[:, i : i + R] for i in range(0, 4 * R, R)], axis=0)
    output_work = eliminate(augmented(gram), 0, 16)
    wide_gather(1)
    output_work = eliminate(output_work, 16, R)
    thin_gather(1)
    query_inverse = query_work[:, R : 2 * R]
    output_inverse = output_work[:, R : 2 * R]
    uq_out[...] = exact(query_inverse, left_query, ((1,), (0,)))
    uo_out[...] = exact(output_inverse, left_output, ((1,), (0,)))
    ro_out[...] = exact(output_inverse, wide_result(1), ((1,), (0,)))
    rq_out[...] = exact(query_inverse, thin_result(1), ((1,), (0,)))

    for p in range(2):
        k = 8 * p
        sent(wide_in.at[p], k)
        sent(wide_z.at[p, pl.ds(0, nz - 1)], k + 1)
        sent(wide_all.at[p, pl.ds(0, nt * nx - 1)], k + 2)
        sent(thin_in.at[p], k + 3)
        sent(thin_z.at[p, pl.ds(0, nz - 1)], k + 4)
        sent(thin_zll.at[p, pl.ds(0, nx - 1)], k + 6)
    sent(gram_all.at[pl.ds(0, nt - 1)], 7)


def stacked(left, right):
    left_high = left.astype(BF16)
    left_low = (left - left_high.astype(F32)).astype(BF16)
    right_high = right.astype(BF16)
    right_low = (right - right_high.astype(F32)).astype(BF16)
    return lax.dot_general(
        jnp.concatenate([left_high, left_low, left_high], axis=0),
        jnp.concatenate([right_high, right_high, right_low], axis=0),
        (((0,), (0,)), ((), ())),
        preferred_element_type=F32,
    )


def finish(
    replicas, uq, rq, uo, ro, gq, eq, go, eo,
    reduced_query, reduced_output, error_query, error_output, right_query, right_output,
):
    scale = 1.0 / replicas
    approx = stacked(uq[...], rq[...])
    reduced_query[...] = approx.astype(BF16)
    error_query[...] = (gq[...].astype(F32) + eq[...].astype(F32) - approx * scale).astype(BF16)
    approx = stacked(uo[...], ro[...])
    reduced_output[...] = approx.astype(BF16)
    error_output[...] = (go[...].astype(F32) + eo[...].astype(F32) - approx * scale).astype(BF16)
    right_query[...] = rq[...]
    right_output[...] = ro[...]


def local(sizes, grad_query, error_query, basis_query, grad_output, error_output, basis_output):
    ny, nc, nx, nz = sizes
    nt = ny * nc
    gq, eq, go, eo = grad_query[0], error_query[0], grad_output[0], error_output[0]
    rows, columns = gq.shape
    hidden, features = go.shape
    part = R // nx
    hbm = pl.BlockSpec(memory_space=pltpu.HBM)
    vmem = pl.BlockSpec(memory_space=pltpu.VMEM)
    shape = jax.ShapeDtypeStruct
    uq, rq, uo, ro = pl.pallas_call(
        functools.partial(exchange, ny, nc, nx, nz),
        out_shape=(
            shape((R, rows), F32), shape((R, columns), F32), shape((R, hidden), F32), shape((R, features), F32),
        ),
        in_specs=[hbm] * 6,
        out_specs=(vmem,) * 4,
        scratch_shapes=[
            pltpu.VMEM((rows, columns), BF16),
            pltpu.VMEM((rows, columns), BF16),
            pltpu.VMEM((R, columns), F32),
            pltpu.VMEM((hidden, features), BF16),
            pltpu.VMEM((hidden, features), BF16),
            pltpu.VMEM((R, features), F32),
            pltpu.SemaphoreType.DMA((6,)),
            pltpu.VMEM((2, nt, nx, part, LANES), F32),
            pltpu.VMEM((2, nt * nx - 1, part, LANES), F32),
            pltpu.VMEM((2, nz, part, LANES), F32),
            pltpu.VMEM((2, nt * nx, part, LANES), F32),
            pltpu.VMEM((2, nx, part, hidden), F32),
            pltpu.VMEM((2, nx - 1, part, hidden), F32),
            pltpu.VMEM((2, nz, part, hidden), F32),
            pltpu.VMEM((2, nx, part, hidden), F32),
            pltpu.VMEM((nt, 8, LANES), F32),
            pltpu.SemaphoreType.DMA((16,)),
            pltpu.SemaphoreType.DMA((16,)),
            pltpu.SemaphoreType.REGULAR,
        ],
        compiler_params=pltpu.CompilerParams(
            collective_id=0, has_side_effects=True, vmem_limit_bytes=60 * 1024 * 1024
        ),
    )(gq, eq, basis_query.T, go, eo, basis_output.T)
    outs = pl.pallas_call(
        functools.partial(finish, nx * nz),
        out_shape=(
            shape((rows, columns), BF16), shape((hidden, features), BF16),
            shape((rows, columns), BF16), shape((hidden, features), BF16),
            shape((R, columns), F32), shape((R, features), F32),
        ),
        grid=(2,),
        in_specs=[
            pl.BlockSpec((R, rows // 2), lambda i: (0, i)),
            pl.BlockSpec((R, columns), lambda i: (0, 0)),
            pl.BlockSpec((R, hidden // 2), lambda i: (0, i)),
            pl.BlockSpec((R, features), lambda i: (0, 0)),
            pl.BlockSpec((rows // 2, columns), lambda i: (i, 0)),
            pl.BlockSpec((rows // 2, columns), lambda i: (i, 0)),
            pl.BlockSpec((hidden // 2, features), lambda i: (i, 0)),
            pl.BlockSpec((hidden // 2, features), lambda i: (i, 0)),
        ],
        out_specs=(
            pl.BlockSpec((rows // 2, columns), lambda i: (i, 0)),
            pl.BlockSpec((hidden // 2, features), lambda i: (i, 0)),
            pl.BlockSpec((rows // 2, columns), lambda i: (i, 0)),
            pl.BlockSpec((hidden // 2, features), lambda i: (i, 0)),
            pl.BlockSpec((R, columns), lambda i: (0, 0)),
            pl.BlockSpec((R, features), lambda i: (0, 0)),
        ),
        compiler_params=pltpu.CompilerParams(vmem_limit_bytes=60 * 1024 * 1024),
    )(uq, rq, uo, ro, gq, eq, go, eo)
    return outs[0], outs[1], outs[2][None], outs[3][None], outs[4].T, outs[5].T


def solution(mesh):
    nt, n = mesh.shape["tensor"], mesh.shape["dp"]
    nx = 4 if n >= 64 else 2
    return jax.shard_map(
        functools.partial(local, (nt // 2, 2, nx, n // nx)),
        mesh=mesh,
        in_specs=(
            P("dp", None, "tensor"),
            P("dp", None, "tensor"),
            P("tensor", None),
            P("dp", "tensor", None),
            P("dp", "tensor", None),
            P(),
        ),
        out_specs=(
            P(None, "tensor"),
            P("tensor", None),
            P("dp", None, "tensor"),
            P("dp", "tensor", None),
            P("tensor", None),
            P(),
        ),
        check_vma=False,
    )
```

```python
import functools

import jax
import jax.numpy as jnp
from jax import lax
from jax.experimental import pallas as pl
from jax.experimental.pallas import tpu as pltpu
from jax.sharding import PartitionSpec as P

MESH = pl.DeviceIdType.MESH
F32 = jnp.float32
BF16 = jnp.bfloat16
R = 32
LANES = 128


def split3(a):
    high = a.astype(BF16)
    rest = a - high.astype(F32)
    middle = rest.astype(BF16)
    low = (rest - middle.astype(F32)).astype(BF16)
    return jnp.concatenate([high, middle, low], axis=0)


def fold3(p):
    return (p[2 * R :] + p[R : 2 * R]) + p[:R]


def rows_by_rows(a, m):
    return lax.dot_general(a, m, (((1,), (1,)), ((), ())), preferred_element_type=F32)


def rows_by_columns(a, m):
    return lax.dot_general(a, m, (((1,), (0,)), ((), ())), preferred_element_type=F32)


def exact(a, b, dims):
    return lax.dot_general(
        a, b, (dims, ((), ())), precision=lax.Precision.HIGHEST, preferred_element_type=F32
    )


def eliminate(works, first, last):
    row = lax.broadcasted_iota(jnp.int32, works[0].shape, 0)
    for j in range(first, last):
        columns = [jnp.broadcast_to(work[:, j : j + 1], work.shape) for work in works]
        inverses = [1.0 / column[j : j + 1] for column in columns]
        scaled = [work[j : j + 1] * inverse for work, inverse in zip(works, inverses)]
        works = [
            jnp.where(row > j, work - column * pivot_row, work)
            for work, column, pivot_row in zip(works, columns, scaled)
        ]
    return works


def lower_inverse(work):
    rows = lax.broadcasted_iota(jnp.int32, (R, R), 0)
    columns = lax.broadcasted_iota(jnp.int32, (R, R), 1)
    pivots = jnp.sum(jnp.where(rows == columns, work[:, :R], 0.0), axis=1, keepdims=True)
    return work[:, R : 2 * R] / jnp.sqrt(pivots)


def augmented(gram):
    rows = lax.broadcasted_iota(jnp.int32, (R, R), 0)
    columns = lax.broadcasted_iota(jnp.int32, (R, R), 1)
    eye = jnp.where(rows == columns, 1.0, 0.0).astype(F32)
    return jnp.concatenate([gram, eye], axis=1)


def exchange(
    ny, nc, nx, nz,
    gq_hbm, eq_hbm, bq_hbm, go_hbm, eo_hbm, bo_hbm,
    uq_out, rq_out, uo_out, ro_out,
    gq, eq, bq, go, eo, bo, load_sem,
    wide_here, wide_in, wide_z, wide_all,
    thin_here, thin_in, thin_z, thin_all,
    gram_all, send_sem, recv_sem, relay_sem,
):
    nt = ny * nc
    part = R // nx
    dp = lax.axis_index("dp")
    t = lax.axis_index("tensor")
    z = dp // nx
    x = lax.rem(dp, nx)
    y = t // nc
    c = lax.rem(t, nc)

    def hops(d, n):
        return min(d, n - d)

    plane = sorted(
        ((dy, dc, dx) for dx in range(nx) for dy in range(ny) for dc in range(nc) if dx or dy or dc),
        key=lambda d: -hops(d[0], ny) - hops(d[2], nx),
    )
    along_z = sorted(range(1, nz), key=lambda d: -hops(d, nz))
    reach = nz // 4
    along_x = sorted(range(1, nx), key=lambda d: -hops(d, nx))

    def turned_t(dy, dc):
        return lax.rem(y + dy, ny) * nc + lax.rem(c + dc, nc)

    def turned_x(dx):
        return lax.rem(x + dx, nx)

    def in_plane(t_, x_):
        return (z * nx + x_, t_)

    def at_z(z_):
        return (z_ * nx + x, t)

    def signal(device):
        pl.semaphore_signal(barrier, inc=1, device_id=device, device_id_type=MESH)

    barrier = pltpu.get_barrier_semaphore()
    for d in along_z:
        if hops(d, nz) <= reach:
            signal(at_z(lax.rem(z + d, nz)))

    loads = []
    for i, (source, target) in enumerate(
        ((bo_hbm, bo), (go_hbm, go), (eo_hbm, eo), (bq_hbm, bq), (gq_hbm, gq), (eq_hbm, eq))
    ):
        copy = pltpu.make_async_copy(source, target, load_sem.at[i])
        copy.start()
        loads.append(copy)

    for dy, dc, dx in plane:
        signal(in_plane(turned_t(dy, dc), turned_x(dx)))

    def remote(source, target, k, device):
        pltpu.make_async_remote_copy(
            src_ref=source, dst_ref=target, send_sem=send_sem.at[k], recv_sem=recv_sem.at[k],
            device_id=device, device_id_type=MESH,
        ).start()

    def arrived(ref, k):
        pltpu.make_async_copy(ref, ref, recv_sem.at[k]).wait()

    def sent(ref, k):
        pltpu.make_async_copy(ref, ref, send_sem.at[k]).wait()

    def total(terms):
        while len(terms) > 1:
            pairs = [terms[i] + terms[i + 1] for i in range(0, len(terms) - 1, 2)]
            terms = pairs + terms[len(pairs) * 2 :]
        return terms[0]

    def wide_scatter(p, value):
        for i in range(nt):
            for j in range(nx):
                wide_here[p, i, j] = value[j * part : (j + 1) * part, i * LANES : (i + 1) * LANES]
        for i, (dy, dc, dx) in enumerate(plane):
            t_, x_ = turned_t(dy, dc), turned_x(dx)
            remote(wide_here.at[p, t_, x_], wide_in.at[p, i], 8 * p, in_plane(t_, x_))

    def wide_exchange(p):
        arrived(wide_in.at[p], 8 * p)
        wide_z[p, z] = total([wide_here[p, t, x]] + [wide_in[p, i] for i in range(len(plane))])
        for d in along_z:
            remote(wide_z.at[p, z], wide_z.at[p, z], 8 * p + 1, at_z(lax.rem(z + d, nz)))

    def wide_gather(p):
        arrived(wide_z.at[p, pl.ds(0, nz - 1)], 8 * p + 1)
        here = t * nx + x
        wide_all[p, here] = total([wide_z[p, i] for i in range(nz)])
        for dy, dc, dx in plane:
            remote(
                wide_all.at[p, here], wide_all.at[p, here], 8 * p + 2, in_plane(turned_t(dy, dc), turned_x(dx))
            )

    def wide_result(p):
        arrived(wide_all.at[p, pl.ds(0, nt * nx - 1)], 8 * p + 2)
        return jnp.concatenate(
            [jnp.concatenate([wide_all[p, i * nx + j] for j in range(nx)], axis=0) for i in range(nt)], axis=1
        )

    def thin_scatter(p, value):
        for j in range(nx):
            thin_here[p, j] = value[j * part : (j + 1) * part]
        for i, dx in enumerate(along_x):
            x_ = turned_x(dx)
            remote(thin_here.at[p, x_], thin_in.at[p, i], 8 * p + 3, in_plane(t, x_))

    def thin_exchange(p):
        arrived(thin_in.at[p], 8 * p + 3)
        thin_z[p, z] = total([thin_here[p, x]] + [thin_in[p, i] for i in range(nx - 1)])
        for d in along_z:
            remote(thin_z.at[p, z], thin_z.at[p, z], 8 * p + 4, at_z(lax.rem(z + d, nz)))

    def thin_gather(p):
        arrived(thin_z.at[p, pl.ds(0, nz - 1)], 8 * p + 4)
        thin_all[p, x] = total([thin_z[p, i] for i in range(nz)])
        for dx in along_x:
            remote(thin_all.at[p, x], thin_all.at[p, x], 8 * p + 6, in_plane(t, turned_x(dx)))

    def thin_result(p):
        arrived(thin_all.at[p, pl.ds(0, nx - 1)], 8 * p + 6)
        return jnp.concatenate([thin_all[p, j] for j in range(nx)], axis=0)

    for i in range(3):
        loads[i].wait()
    terms = split3(bo[...])
    value = fold3(rows_by_rows(terms, go[...]) + rows_by_rows(terms, eo[...]))
    pl.semaphore_wait(barrier, len(plane) + 2 * reach)
    for d in (reach, nz - reach):
        pl.semaphore_signal(relay_sem, inc=1, device_id=at_z(lax.rem(z + d, nz)), device_id_type=MESH)
    thin_scatter(0, value)
    for i in range(3, 6):
        loads[i].wait()
    terms = split3(bq[...])
    value = fold3(rows_by_rows(terms, gq[...]) + rows_by_rows(terms, eq[...]))
    wide_scatter(0, value)
    pl.semaphore_wait(relay_sem, 2)
    thin_exchange(0)
    wide_exchange(0)
    thin_gather(0)
    wide_gather(0)

    left_output = thin_result(0)
    terms = split3(left_output)
    value = fold3(rows_by_columns(terms, go[...]) + rows_by_columns(terms, eo[...]))
    wide_scatter(1, value)
    gram = exact(left_output, left_output, ((1,), (1,)))
    gram_all[t] = jnp.concatenate([gram[i : i + 8] for i in range(0, R, 8)], axis=1)
    for dy, dc, dx in plane:
        if dx == 0:
            remote(gram_all.at[t], gram_all.at[t], 7, in_plane(turned_t(dy, dc), x))
    left_query = wide_result(0)
    terms = split3(left_query)
    value = fold3(rows_by_columns(terms, gq[...]) + rows_by_columns(terms, eq[...]))
    thin_scatter(1, value)
    query_gram = exact(left_query, left_query, ((1,), (1,)))
    wide_exchange(1)
    thin_exchange(1)
    arrived(gram_all.at[pl.ds(0, nt - 1)], 7)
    gram = total([gram_all[i] for i in range(nt)])
    gram = jnp.concatenate([gram[:, i : i + R] for i in range(0, 4 * R, R)], axis=0)
    works = eliminate([augmented(query_gram), augmented(gram)], 0, R)
    query_inverse, output_inverse = [lower_inverse(work) for work in works]
    wide_gather(1)
    thin_gather(1)
    uq_out[...] = exact(query_inverse, left_query, ((1,), (0,)))
    uo_out[...] = exact(output_inverse, left_output, ((1,), (0,)))
    ro_out[...] = exact(output_inverse, wide_result(1), ((1,), (0,)))
    rq_out[...] = exact(query_inverse, thin_result(1), ((1,), (0,)))

    for p in range(2):
        k = 8 * p
        sent(wide_in.at[p], k)
        sent(wide_z.at[p, pl.ds(0, nz - 1)], k + 1)
        sent(wide_all.at[p, pl.ds(0, nt * nx - 1)], k + 2)
        sent(thin_in.at[p], k + 3)
        sent(thin_z.at[p, pl.ds(0, nz - 1)], k + 4)
        sent(thin_all.at[p, pl.ds(0, nx - 1)], k + 6)
    sent(gram_all.at[pl.ds(0, nt - 1)], 7)


def stacked(left, right):
    left_high = left.astype(BF16)
    left_low = (left - left_high.astype(F32)).astype(BF16)
    right_high = right.astype(BF16)
    right_low = (right - right_high.astype(F32)).astype(BF16)
    return lax.dot_general(
        jnp.concatenate([left_high, left_low, left_high], axis=0),
        jnp.concatenate([right_high, right_high, right_low], axis=0),
        (((0,), (0,)), ((), ())),
        preferred_element_type=F32,
    )


def finish(
    replicas, uq, rq, uo, ro, gq, eq, go, eo,
    reduced_query, reduced_output, error_query, error_output, right_query, right_output,
):
    scale = 1.0 / replicas
    approx = stacked(uq[...], rq[...])
    reduced_query[...] = approx.astype(BF16)
    error_query[...] = (gq[...].astype(F32) + eq[...].astype(F32) - approx * scale).astype(BF16)
    approx = stacked(uo[...], ro[...])
    reduced_output[...] = approx.astype(BF16)
    error_output[...] = (go[...].astype(F32) + eo[...].astype(F32) - approx * scale).astype(BF16)
    right_query[...] = rq[...]
    right_output[...] = ro[...]


def local(sizes, grad_query, error_query, basis_query, grad_output, error_output, basis_output):
    ny, nc, nx, nz = sizes
    nt = ny * nc
    gq, eq, go, eo = grad_query[0], error_query[0], grad_output[0], error_output[0]
    rows, columns = gq.shape
    hidden, features = go.shape
    part = R // nx
    hbm = pl.BlockSpec(memory_space=pltpu.HBM)
    vmem = pl.BlockSpec(memory_space=pltpu.VMEM)
    shape = jax.ShapeDtypeStruct
    uq, rq, uo, ro = pl.pallas_call(
        functools.partial(exchange, ny, nc, nx, nz),
        out_shape=(
            shape((R, rows), F32), shape((R, columns), F32), shape((R, hidden), F32), shape((R, features), F32),
        ),
        in_specs=[hbm] * 6,
        out_specs=(vmem,) * 4,
        scratch_shapes=[
            pltpu.VMEM((rows, columns), BF16),
            pltpu.VMEM((rows, columns), BF16),
            pltpu.VMEM((R, columns), F32),
            pltpu.VMEM((hidden, features), BF16),
            pltpu.VMEM((hidden, features), BF16),
            pltpu.VMEM((R, features), F32),
            pltpu.SemaphoreType.DMA((6,)),
            pltpu.VMEM((2, nt, nx, part, LANES), F32),
            pltpu.VMEM((2, nt * nx - 1, part, LANES), F32),
            pltpu.VMEM((2, nz, part, LANES), F32),
            pltpu.VMEM((2, nt * nx, part, LANES), F32),
            pltpu.VMEM((2, nx, part, hidden), F32),
            pltpu.VMEM((2, nx - 1, part, hidden), F32),
            pltpu.VMEM((2, nz, part, hidden), F32),
            pltpu.VMEM((2, nx, part, hidden), F32),
            pltpu.VMEM((nt, 8, LANES), F32),
            pltpu.SemaphoreType.DMA((16,)),
            pltpu.SemaphoreType.DMA((16,)),
            pltpu.SemaphoreType.REGULAR,
        ],
        compiler_params=pltpu.CompilerParams(
            collective_id=0, has_side_effects=True, vmem_limit_bytes=60 * 1024 * 1024
        ),
    )(gq, eq, basis_query.T, go, eo, basis_output.T)
    outs = pl.pallas_call(
        functools.partial(finish, nx * nz),
        out_shape=(
            shape((rows, columns), BF16), shape((hidden, features), BF16),
            shape((rows, columns), BF16), shape((hidden, features), BF16),
            shape((R, columns), F32), shape((R, features), F32),
        ),
        grid=(2,),
        in_specs=[
            pl.BlockSpec((R, rows // 2), lambda i: (0, i)),
            pl.BlockSpec((R, columns), lambda i: (0, 0)),
            pl.BlockSpec((R, hidden // 2), lambda i: (0, i)),
            pl.BlockSpec((R, features), lambda i: (0, 0)),
            pl.BlockSpec((rows // 2, columns), lambda i: (i, 0)),
            pl.BlockSpec((rows // 2, columns), lambda i: (i, 0)),
            pl.BlockSpec((hidden // 2, features), lambda i: (i, 0)),
            pl.BlockSpec((hidden // 2, features), lambda i: (i, 0)),
        ],
        out_specs=(
            pl.BlockSpec((rows // 2, columns), lambda i: (i, 0)),
            pl.BlockSpec((hidden // 2, features), lambda i: (i, 0)),
            pl.BlockSpec((rows // 2, columns), lambda i: (i, 0)),
            pl.BlockSpec((hidden // 2, features), lambda i: (i, 0)),
            pl.BlockSpec((R, columns), lambda i: (0, 0)),
            pl.BlockSpec((R, features), lambda i: (0, 0)),
        ),
        compiler_params=pltpu.CompilerParams(vmem_limit_bytes=60 * 1024 * 1024),
    )(uq, rq, uo, ro, gq, eq, go, eo)
    return outs[0], outs[1], outs[2][None], outs[3][None], outs[4].T, outs[5].T


def solution(mesh):
    nt, n = mesh.shape["tensor"], mesh.shape["dp"]
    nx = 4 if n >= 64 else 2
    return jax.shard_map(
        functools.partial(local, (nt // 2, 2, nx, n // nx)),
        mesh=mesh,
        in_specs=(
            P("dp", None, "tensor"),
            P("dp", None, "tensor"),
            P("tensor", None),
            P("dp", "tensor", None),
            P("dp", "tensor", None),
            P(),
        ),
        out_specs=(
            P(None, "tensor"),
            P("tensor", None),
            P("dp", None, "tensor"),
            P("dp", "tensor", None),
            P("tensor", None),
            P(),
        ),
        check_vma=False,
    )
```

```python
import functools

import jax
import jax.numpy as jnp
from jax import lax
from jax.experimental import pallas as pl
from jax.experimental.pallas import tpu as pltpu
from jax.sharding import PartitionSpec as P

MESH = pl.DeviceIdType.MESH
F32 = jnp.float32
BF16 = jnp.bfloat16
R = 32
LANES = 128


def split3(a):
    high = a.astype(BF16)
    rest = a - high.astype(F32)
    middle = rest.astype(BF16)
    low = (rest - middle.astype(F32)).astype(BF16)
    return jnp.concatenate([high, middle, low], axis=0)


def fold3(p):
    return (p[2 * R :] + p[R : 2 * R]) + p[:R]


def rows_by_rows(a, m):
    return lax.dot_general(a, m, (((1,), (1,)), ((), ())), preferred_element_type=F32)


def rows_by_columns(a, m):
    return lax.dot_general(a, m, (((1,), (0,)), ((), ())), preferred_element_type=F32)


def exact(a, b, dims):
    return lax.dot_general(
        a, b, (dims, ((), ())), precision=lax.Precision.HIGHEST, preferred_element_type=F32
    )


def eliminate(works, first, last):
    row = lax.broadcasted_iota(jnp.int32, works[0].shape, 0)
    for j in range(first, last):
        columns = [jnp.broadcast_to(work[:, j : j + 1], work.shape) for work in works]
        inverses = [1.0 / column[j : j + 1] for column in columns]
        scaled = [work[j : j + 1] * inverse for work, inverse in zip(works, inverses)]
        works = [
            jnp.where(row > j, work - column * pivot_row, work)
            for work, column, pivot_row in zip(works, columns, scaled)
        ]
    return works


def lower_inverse(work):
    rows = lax.broadcasted_iota(jnp.int32, (R, R), 0)
    columns = lax.broadcasted_iota(jnp.int32, (R, R), 1)
    pivots = jnp.sum(jnp.where(rows == columns, work[:, :R], 0.0), axis=1, keepdims=True)
    return work[:, R : 2 * R] / jnp.sqrt(pivots)


def augmented(gram):
    rows = lax.broadcasted_iota(jnp.int32, (R, R), 0)
    columns = lax.broadcasted_iota(jnp.int32, (R, R), 1)
    eye = jnp.where(rows == columns, 1.0, 0.0).astype(F32)
    return jnp.concatenate([gram, eye], axis=1)


def exchange(
    ny, nc, nx, nz,
    gq_hbm, eq_hbm, bq_hbm, go_hbm, eo_hbm, bo_hbm,
    uq_out, rq_out, uo_out, ro_out, gq, eq, go, eo,
    bq, bo, load_sem,
    wide_here, wide_in, wide_z, wide_all,
    thin_here, thin_in, thin_z, thin_all,
    gram_all, send_sem, recv_sem, relay_sem,
):
    nt = ny * nc
    part = R // nx
    dp = lax.axis_index("dp")
    t = lax.axis_index("tensor")
    z = dp // nx
    x = lax.rem(dp, nx)
    y = t // nc
    c = lax.rem(t, nc)

    def hops(d, n):
        return min(d, n - d)

    plane = sorted(
        ((dy, dc, dx) for dx in range(nx) for dy in range(ny) for dc in range(nc) if dx or dy or dc),
        key=lambda d: -hops(d[0], ny) - hops(d[2], nx),
    )
    along_z = sorted(range(1, nz), key=lambda d: -hops(d, nz))
    reach = nz // 4
    along_x = sorted(range(1, nx), key=lambda d: -hops(d, nx))

    def turned_t(dy, dc):
        return lax.rem(y + dy, ny) * nc + lax.rem(c + dc, nc)

    def turned_x(dx):
        return lax.rem(x + dx, nx)

    def in_plane(t_, x_):
        return (z * nx + x_, t_)

    def at_z(z_):
        return (z_ * nx + x, t)

    def signal(device):
        pl.semaphore_signal(barrier, inc=1, device_id=device, device_id_type=MESH)

    barrier = pltpu.get_barrier_semaphore()
    for d in along_z:
        if hops(d, nz) <= reach:
            signal(at_z(lax.rem(z + d, nz)))

    loads = []
    for i, (source, target) in enumerate(
        ((bo_hbm, bo), (go_hbm, go), (eo_hbm, eo), (bq_hbm, bq), (gq_hbm, gq), (eq_hbm, eq))
    ):
        copy = pltpu.make_async_copy(source, target, load_sem.at[i])
        copy.start()
        loads.append(copy)

    for dy, dc, dx in plane:
        signal(in_plane(turned_t(dy, dc), turned_x(dx)))

    def remote(source, target, k, device):
        pltpu.make_async_remote_copy(
            src_ref=source, dst_ref=target, send_sem=send_sem.at[k], recv_sem=recv_sem.at[k],
            device_id=device, device_id_type=MESH,
        ).start()

    def arrived(ref, k):
        pltpu.make_async_copy(ref, ref, recv_sem.at[k]).wait()

    def sent(ref, k):
        pltpu.make_async_copy(ref, ref, send_sem.at[k]).wait()

    def total(terms):
        while len(terms) > 1:
            pairs = [terms[i] + terms[i + 1] for i in range(0, len(terms) - 1, 2)]
            terms = pairs + terms[len(pairs) * 2 :]
        return terms[0]

    def wide_scatter(p, value):
        for i in range(nt):
            for j in range(nx):
                wide_here[p, i, j] = value[j * part : (j + 1) * part, i * LANES : (i + 1) * LANES]
        for i, (dy, dc, dx) in enumerate(plane):
            t_, x_ = turned_t(dy, dc), turned_x(dx)
            remote(wide_here.at[p, t_, x_], wide_in.at[p, i], 8 * p, in_plane(t_, x_))

    def wide_exchange(p):
        arrived(wide_in.at[p], 8 * p)
        wide_z[p, z] = total([wide_here[p, t, x]] + [wide_in[p, i] for i in range(len(plane))])
        for d in along_z:
            remote(wide_z.at[p, z], wide_z.at[p, z], 8 * p + 1, at_z(lax.rem(z + d, nz)))

    def wide_gather(p):
        arrived(wide_z.at[p, pl.ds(0, nz - 1)], 8 * p + 1)
        here = t * nx + x
        wide_all[p, here] = total([wide_z[p, i] for i in range(nz)])
        for dy, dc, dx in plane:
            remote(
                wide_all.at[p, here], wide_all.at[p, here], 8 * p + 2, in_plane(turned_t(dy, dc), turned_x(dx))
            )

    def wide_result(p):
        arrived(wide_all.at[p, pl.ds(0, nt * nx - 1)], 8 * p + 2)
        return jnp.concatenate(
            [jnp.concatenate([wide_all[p, i * nx + j] for j in range(nx)], axis=0) for i in range(nt)], axis=1
        )

    def thin_scatter(p, value):
        for j in range(nx):
            thin_here[p, j] = value[j * part : (j + 1) * part]
        for i, dx in enumerate(along_x):
            x_ = turned_x(dx)
            remote(thin_here.at[p, x_], thin_in.at[p, i], 8 * p + 3, in_plane(t, x_))

    def thin_exchange(p):
        arrived(thin_in.at[p], 8 * p + 3)
        thin_z[p, z] = total([thin_here[p, x]] + [thin_in[p, i] for i in range(nx - 1)])
        for d in along_z:
            remote(thin_z.at[p, z], thin_z.at[p, z], 8 * p + 4, at_z(lax.rem(z + d, nz)))

    def thin_gather(p):
        arrived(thin_z.at[p, pl.ds(0, nz - 1)], 8 * p + 4)
        thin_all[p, x] = total([thin_z[p, i] for i in range(nz)])
        for dx in along_x:
            remote(thin_all.at[p, x], thin_all.at[p, x], 8 * p + 6, in_plane(t, turned_x(dx)))

    def thin_result(p):
        arrived(thin_all.at[p, pl.ds(0, nx - 1)], 8 * p + 6)
        return jnp.concatenate([thin_all[p, j] for j in range(nx)], axis=0)

    for i in range(3):
        loads[i].wait()
    terms = split3(bo[...])
    value = fold3(rows_by_rows(terms, go[...]) + rows_by_rows(terms, eo[...]))
    pl.semaphore_wait(barrier, len(plane) + 2 * reach)
    for d in (reach, nz - reach):
        pl.semaphore_signal(relay_sem, inc=1, device_id=at_z(lax.rem(z + d, nz)), device_id_type=MESH)
    thin_scatter(0, value)
    for i in range(3, 6):
        loads[i].wait()
    terms = split3(bq[...])
    value = fold3(rows_by_rows(terms, gq[...]) + rows_by_rows(terms, eq[...]))
    wide_scatter(0, value)
    pl.semaphore_wait(relay_sem, 2)
    thin_exchange(0)
    wide_exchange(0)
    thin_gather(0)
    wide_gather(0)

    left_output = thin_result(0)
    terms = split3(left_output)
    value = fold3(rows_by_columns(terms, go[...]) + rows_by_columns(terms, eo[...]))
    wide_scatter(1, value)
    gram = exact(left_output, left_output, ((1,), (1,)))
    gram_all[t] = jnp.concatenate([gram[i : i + 8] for i in range(0, R, 8)], axis=1)
    for dy, dc, dx in plane:
        if dx == 0:
            remote(gram_all.at[t], gram_all.at[t], 7, in_plane(turned_t(dy, dc), x))
    left_query = wide_result(0)
    terms = split3(left_query)
    value = fold3(rows_by_columns(terms, gq[...]) + rows_by_columns(terms, eq[...]))
    thin_scatter(1, value)
    query_gram = exact(left_query, left_query, ((1,), (1,)))
    wide_exchange(1)
    thin_exchange(1)
    arrived(gram_all.at[pl.ds(0, nt - 1)], 7)
    gram = total([gram_all[i] for i in range(nt)])
    gram = jnp.concatenate([gram[:, i : i + R] for i in range(0, 4 * R, R)], axis=0)
    works = eliminate([augmented(query_gram), augmented(gram)], 0, R)
    query_inverse, output_inverse = [lower_inverse(work) for work in works]
    wide_gather(1)
    thin_gather(1)
    uq_out[...] = exact(query_inverse, left_query, ((1,), (0,)))
    uo_out[...] = exact(output_inverse, left_output, ((1,), (0,)))
    ro_out[...] = exact(output_inverse, wide_result(1), ((1,), (0,)))
    rq_out[...] = exact(query_inverse, thin_result(1), ((1,), (0,)))

    for p in range(2):
        k = 8 * p
        sent(wide_in.at[p], k)
        sent(wide_z.at[p, pl.ds(0, nz - 1)], k + 1)
        sent(wide_all.at[p, pl.ds(0, nt * nx - 1)], k + 2)
        sent(thin_in.at[p], k + 3)
        sent(thin_z.at[p, pl.ds(0, nz - 1)], k + 4)
        sent(thin_all.at[p, pl.ds(0, nx - 1)], k + 6)
    sent(gram_all.at[pl.ds(0, nt - 1)], 7)


def stacked(left, right):
    left_high = left.astype(BF16)
    left_low = (left - left_high.astype(F32)).astype(BF16)
    right_high = right.astype(BF16)
    right_low = (right - right_high.astype(F32)).astype(BF16)
    return lax.dot_general(
        jnp.concatenate([left_high, left_low, left_high], axis=0),
        jnp.concatenate([right_high, right_high, right_low], axis=0),
        (((0,), (0,)), ((), ())),
        preferred_element_type=F32,
    )


def finish(
    replicas, uq, rq, uo, ro, gq, eq, go, eo,
    reduced_query, reduced_output, error_query, error_output, right_query, right_output,
):
    scale = 1.0 / replicas
    approx = stacked(uq[...], rq[...])
    reduced_query[...] = approx.astype(BF16)
    error_query[...] = (gq[...].astype(F32) + eq[...].astype(F32) - approx * scale).astype(BF16)
    approx = stacked(uo[...], ro[...])
    reduced_output[...] = approx.astype(BF16)
    error_output[...] = (go[...].astype(F32) + eo[...].astype(F32) - approx * scale).astype(BF16)
    right_query[...] = rq[...]
    right_output[...] = ro[...]


def local(sizes, grad_query, error_query, basis_query, grad_output, error_output, basis_output):
    ny, nc, nx, nz = sizes
    nt = ny * nc
    gq, eq, go, eo = grad_query[0], error_query[0], grad_output[0], error_output[0]
    rows, columns = gq.shape
    hidden, features = go.shape
    part = R // nx
    hbm = pl.BlockSpec(memory_space=pltpu.HBM)
    vmem = pl.BlockSpec(memory_space=pltpu.VMEM)
    shape = jax.ShapeDtypeStruct
    uq, rq, uo, ro, gq, eq, go, eo = pl.pallas_call(
        functools.partial(exchange, ny, nc, nx, nz),
        out_shape=(
            shape((R, rows), F32), shape((R, columns), F32), shape((R, hidden), F32), shape((R, features), F32),
            shape((rows, columns), BF16), shape((rows, columns), BF16),
            shape((hidden, features), BF16), shape((hidden, features), BF16),
        ),
        in_specs=[hbm] * 6,
        out_specs=(vmem,) * 8,
        scratch_shapes=[
            pltpu.VMEM((R, columns), F32),
            pltpu.VMEM((R, features), F32),
            pltpu.SemaphoreType.DMA((6,)),
            pltpu.VMEM((2, nt, nx, part, LANES), F32),
            pltpu.VMEM((2, nt * nx - 1, part, LANES), F32),
            pltpu.VMEM((2, nz, part, LANES), F32),
            pltpu.VMEM((2, nt * nx, part, LANES), F32),
            pltpu.VMEM((2, nx, part, hidden), F32),
            pltpu.VMEM((2, nx - 1, part, hidden), F32),
            pltpu.VMEM((2, nz, part, hidden), F32),
            pltpu.VMEM((2, nx, part, hidden), F32),
            pltpu.VMEM((nt, 8, LANES), F32),
            pltpu.SemaphoreType.DMA((16,)),
            pltpu.SemaphoreType.DMA((16,)),
            pltpu.SemaphoreType.REGULAR,
        ],
        compiler_params=pltpu.CompilerParams(
            collective_id=0, has_side_effects=True, vmem_limit_bytes=24576 * 1024
        ),
    )(*(pltpu.with_memory_space_constraint(i, pltpu.HBM) for i in (gq, eq, basis_query.T, go, eo, basis_output.T)))
    outs = pl.pallas_call(
        functools.partial(finish, nx * nz),
        out_shape=(
            shape((rows, columns), BF16), shape((hidden, features), BF16),
            shape((rows, columns), BF16), shape((hidden, features), BF16),
            shape((R, columns), F32), shape((R, features), F32),
        ),
        in_specs=[vmem] * 8,
        out_specs=(vmem,) * 6,
        compiler_params=pltpu.CompilerParams(vmem_limit_bytes=24 * 1024 * 1024),
    )(uq, rq, uo, ro, gq, eq, go, eo)
    return outs[0], outs[1], outs[2][None], outs[3][None], outs[4].T, outs[5].T


def solution(mesh):
    nt, n = mesh.shape["tensor"], mesh.shape["dp"]
    nx = 4 if n >= 64 else 2
    return jax.shard_map(
        functools.partial(local, (nt // 2, 2, nx, n // nx)),
        mesh=mesh,
        in_specs=(
            P("dp", None, "tensor"),
            P("dp", None, "tensor"),
            P("tensor", None),
            P("dp", "tensor", None),
            P("dp", "tensor", None),
            P(),
        ),
        out_specs=(
            P(None, "tensor"),
            P("tensor", None),
            P("dp", None, "tensor"),
            P("dp", "tensor", None),
            P("tensor", None),
            P(),
        ),
        check_vma=False,
    )
```

```python
import functools

import jax
import jax.numpy as jnp
from jax import lax
from jax.experimental import pallas as pl
from jax.experimental.pallas import tpu as pltpu
from jax.sharding import PartitionSpec as P

MESH = pl.DeviceIdType.MESH
F32 = jnp.float32
BF16 = jnp.bfloat16
R = 32
LANES = 128


def split3(a):
    high = a.astype(BF16)
    rest = a - high.astype(F32)
    middle = rest.astype(BF16)
    low = (rest - middle.astype(F32)).astype(BF16)
    return jnp.concatenate([high, middle, low], axis=0)


def fold3(p):
    return (p[2 * R :] + p[R : 2 * R]) + p[:R]


def rows_by_rows(a, m):
    return lax.dot_general(a, m, (((1,), (1,)), ((), ())), preferred_element_type=F32)


def rows_by_columns(a, m):
    return lax.dot_general(a, m, (((1,), (0,)), ((), ())), preferred_element_type=F32)


def exact(a, b, dims):
    return lax.dot_general(
        a, b, (dims, ((), ())), precision=lax.Precision.HIGHEST, preferred_element_type=F32
    )


def eliminate(works, first, last):
    row = lax.broadcasted_iota(jnp.int32, works[0].shape, 0)
    for j in range(first, last):
        columns = [jnp.broadcast_to(work[:, j : j + 1], work.shape) for work in works]
        inverses = [1.0 / column[j : j + 1] for column in columns]
        scaled = [work[j : j + 1] * inverse for work, inverse in zip(works, inverses)]
        works = [
            jnp.where(row > j, work - column * pivot_row, work)
            for work, column, pivot_row in zip(works, columns, scaled)
        ]
    return works


def lower_inverse(work):
    rows = lax.broadcasted_iota(jnp.int32, (R, R), 0)
    columns = lax.broadcasted_iota(jnp.int32, (R, R), 1)
    pivots = jnp.sum(jnp.where(rows == columns, work[:, :R], 0.0), axis=1, keepdims=True)
    return work[:, R : 2 * R] / jnp.sqrt(pivots)


def augmented(gram):
    rows = lax.broadcasted_iota(jnp.int32, (R, R), 0)
    columns = lax.broadcasted_iota(jnp.int32, (R, R), 1)
    eye = jnp.where(rows == columns, 1.0, 0.0).astype(F32)
    return jnp.concatenate([gram, eye], axis=1)


def exchange(
    ny, nc, nx, nz,
    gq_hbm, eq_hbm, bq_hbm, go_hbm, eo_hbm, bo_hbm,
    uq_out, rq_out, uo_out, ro_out, gq, eq, go, eo,
    bq, bo, load_sem,
    wide_here, wide_in, wide_z, wide_all,
    thin_here, thin_in, thin_z, thin_all,
    gram_all, send_sem, recv_sem, relay_sem,
):
    nt = ny * nc
    part = R // nx
    dp = lax.axis_index("dp")
    t = lax.axis_index("tensor")
    z = dp // nx
    x = lax.rem(dp, nx)
    y = t // nc
    c = lax.rem(t, nc)

    def hops(d, n):
        return min(d, n - d)

    plane = sorted(
        ((dy, dc, dx) for dx in range(nx) for dy in range(ny) for dc in range(nc) if dx or dy or dc),
        key=lambda d: -hops(d[0], ny) - hops(d[2], nx),
    )
    along_z = sorted(range(1, nz), key=lambda d: -hops(d, nz))
    reach = nz // 4
    along_x = sorted(range(1, nx), key=lambda d: -hops(d, nx))

    def turned_t(dy, dc):
        return lax.rem(y + dy, ny) * nc + lax.rem(c + dc, nc)

    def turned_x(dx):
        return lax.rem(x + dx, nx)

    def in_plane(t_, x_):
        return (z * nx + x_, t_)

    def at_z(z_):
        return (z_ * nx + x, t)

    def signal(device):
        pl.semaphore_signal(barrier, inc=1, device_id=device, device_id_type=MESH)

    barrier = pltpu.get_barrier_semaphore()
    for d in along_z:
        if hops(d, nz) <= reach:
            signal(at_z(lax.rem(z + d, nz)))

    loads = []
    for i, (source, target) in enumerate(
        ((bo_hbm, bo), (go_hbm, go), (eo_hbm, eo), (bq_hbm, bq), (gq_hbm, gq), (eq_hbm, eq))
    ):
        copy = pltpu.make_async_copy(source, target, load_sem.at[i])
        copy.start()
        loads.append(copy)

    for dy, dc, dx in plane:
        signal(in_plane(turned_t(dy, dc), turned_x(dx)))

    def remote(source, target, k, device):
        pltpu.make_async_remote_copy(
            src_ref=source, dst_ref=target, send_sem=send_sem.at[k], recv_sem=recv_sem.at[k],
            device_id=device, device_id_type=MESH,
        ).start()

    def arrived(ref, k):
        pltpu.make_async_copy(ref, ref, recv_sem.at[k]).wait()

    def sent(ref, k):
        pltpu.make_async_copy(ref, ref, send_sem.at[k]).wait()

    def total(terms):
        while len(terms) > 1:
            pairs = [terms[i] + terms[i + 1] for i in range(0, len(terms) - 1, 2)]
            terms = pairs + terms[len(pairs) * 2 :]
        return terms[0]

    def wide_scatter(p, value):
        for i in range(nt):
            for j in range(nx):
                wide_here[p, i, j] = value[j * part : (j + 1) * part, i * LANES : (i + 1) * LANES]
        for i, (dy, dc, dx) in enumerate(plane):
            t_, x_ = turned_t(dy, dc), turned_x(dx)
            remote(wide_here.at[p, t_, x_], wide_in.at[p, i], 8 * p, in_plane(t_, x_))

    def wide_exchange(p):
        arrived(wide_in.at[p], 8 * p)
        wide_z[p, z] = total([wide_here[p, t, x]] + [wide_in[p, i] for i in range(len(plane))])
        for d in along_z:
            remote(wide_z.at[p, z], wide_z.at[p, z], 8 * p + 1, at_z(lax.rem(z + d, nz)))

    def wide_gather(p):
        arrived(wide_z.at[p, pl.ds(0, nz - 1)], 8 * p + 1)
        here = t * nx + x
        wide_all[p, here] = total([wide_z[p, i] for i in range(nz)])
        for dy, dc, dx in plane:
            remote(
                wide_all.at[p, here], wide_all.at[p, here], 8 * p + 2, in_plane(turned_t(dy, dc), turned_x(dx))
            )

    def wide_result(p):
        arrived(wide_all.at[p, pl.ds(0, nt * nx - 1)], 8 * p + 2)
        return jnp.concatenate(
            [jnp.concatenate([wide_all[p, i * nx + j] for j in range(nx)], axis=0) for i in range(nt)], axis=1
        )

    def thin_scatter(p, value):
        for j in range(nx):
            thin_here[p, j] = value[j * part : (j + 1) * part]
        for i, dx in enumerate(along_x):
            x_ = turned_x(dx)
            remote(thin_here.at[p, x_], thin_in.at[p, i], 8 * p + 3, in_plane(t, x_))

    def thin_exchange(p):
        arrived(thin_in.at[p], 8 * p + 3)
        thin_z[p, z] = total([thin_here[p, x]] + [thin_in[p, i] for i in range(nx - 1)])
        for d in along_z:
            remote(thin_z.at[p, z], thin_z.at[p, z], 8 * p + 4, at_z(lax.rem(z + d, nz)))

    def thin_gather(p):
        arrived(thin_z.at[p, pl.ds(0, nz - 1)], 8 * p + 4)
        thin_all[p, x] = total([thin_z[p, i] for i in range(nz)])
        for dx in along_x:
            remote(thin_all.at[p, x], thin_all.at[p, x], 8 * p + 6, in_plane(t, turned_x(dx)))

    def thin_result(p):
        arrived(thin_all.at[p, pl.ds(0, nx - 1)], 8 * p + 6)
        return jnp.concatenate([thin_all[p, j] for j in range(nx)], axis=0)

    for i in range(3):
        loads[i].wait()
    terms = split3(bo[...])
    value = fold3(rows_by_rows(terms, go[...]) + rows_by_rows(terms, eo[...]))
    pl.semaphore_wait(barrier, len(plane) + 2 * reach)
    for d in (reach, nz - reach):
        pl.semaphore_signal(relay_sem, inc=1, device_id=at_z(lax.rem(z + d, nz)), device_id_type=MESH)
    thin_scatter(0, value)
    for i in range(3, 6):
        loads[i].wait()
    terms = split3(bq[...])
    value = fold3(rows_by_rows(terms, gq[...]) + rows_by_rows(terms, eq[...]))
    wide_scatter(0, value)
    pl.semaphore_wait(relay_sem, 2)
    thin_exchange(0)
    wide_exchange(0)
    thin_gather(0)
    wide_gather(0)

    left_output = thin_result(0)
    terms = split3(left_output)
    value = fold3(rows_by_columns(terms, go[...]) + rows_by_columns(terms, eo[...]))
    wide_scatter(1, value)
    gram = exact(left_output, left_output, ((1,), (1,)))
    gram_all[t] = jnp.concatenate([gram[i : i + 8] for i in range(0, R, 8)], axis=1)
    for dy, dc, dx in plane:
        if dx == 0:
            remote(gram_all.at[t], gram_all.at[t], 7, in_plane(turned_t(dy, dc), x))
    left_query = wide_result(0)
    terms = split3(left_query)
    value = fold3(rows_by_columns(terms, gq[...]) + rows_by_columns(terms, eq[...]))
    thin_scatter(1, value)
    query_gram = exact(left_query, left_query, ((1,), (1,)))
    wide_exchange(1)
    thin_exchange(1)
    arrived(gram_all.at[pl.ds(0, nt - 1)], 7)
    gram = total([gram_all[i] for i in range(nt)])
    gram = jnp.concatenate([gram[:, i : i + R] for i in range(0, 4 * R, R)], axis=0)
    works = eliminate([augmented(query_gram), augmented(gram)], 0, R)
    query_inverse, output_inverse = [lower_inverse(work) for work in works]
    wide_gather(1)
    thin_gather(1)
    uq_out[...] = exact(query_inverse, left_query, ((1,), (0,)))
    uo_out[...] = exact(output_inverse, left_output, ((1,), (0,)))
    ro_out[...] = exact(output_inverse, wide_result(1), ((1,), (0,)))
    rq_out[...] = exact(query_inverse, thin_result(1), ((1,), (0,)))

    for p in range(2):
        k = 8 * p
        sent(wide_in.at[p], k)
        sent(wide_z.at[p, pl.ds(0, nz - 1)], k + 1)
        sent(wide_all.at[p, pl.ds(0, nt * nx - 1)], k + 2)
        sent(thin_in.at[p], k + 3)
        sent(thin_z.at[p, pl.ds(0, nz - 1)], k + 4)
        sent(thin_all.at[p, pl.ds(0, nx - 1)], k + 6)
    sent(gram_all.at[pl.ds(0, nt - 1)], 7)


def finish(
    replicas, parts, uq, rq, uo, ro, gq, eq, go, eo,
    reduced_query, reduced_output, error_query, error_output, right_query, right_output,
    rounded_query, rounded_output, next_query, next_output, sem,
):
    copies = []

    def store(source, target):
        copy = pltpu.make_async_copy(source, target, sem.at[len(copies)])
        copy.start()
        copies.append(copy)

    store(ro, right_output)
    store(rq, right_query)
    scale = 1.0 / replicas
    for u, r, g, e, rounded, following, reduced, error in (
        (uq, rq, gq, eq, rounded_query, next_query, reduced_query, error_query),
        (uo, ro, go, eo, rounded_output, next_output, reduced_output, error_output),
    ):
        left, right = u[...], r[...]
        left_high, right_high = left.astype(BF16), right.astype(BF16)
        left_low = (left - left_high.astype(F32)).astype(BF16)
        right_low = (right - right_high.astype(F32)).astype(BF16)
        left = jnp.concatenate([left_high, left_low, left_high], axis=0)
        right = jnp.concatenate([right_high, right_high, right_low], axis=0)
        rows = g.shape[0] // parts
        for i in range(parts):
            at = pl.ds(i * rows, rows)
            approx = lax.dot_general(
                left[:, i * rows : (i + 1) * rows], right, (((0,), (0,)), ((), ())), preferred_element_type=F32
            )
            rounded[at] = approx.astype(BF16)
            following[at] = (g[at].astype(F32) + e[at].astype(F32) - approx * scale).astype(BF16)
            store(rounded.at[at], reduced.at[at])
            store(following.at[at], error.at[at])
    for copy in copies:
        copy.wait()


def local(sizes, grad_query, error_query, basis_query, grad_output, error_output, basis_output):
    ny, nc, nx, nz = sizes
    nt = ny * nc
    gq, eq, go, eo = grad_query[0], error_query[0], grad_output[0], error_output[0]
    rows, columns = gq.shape
    hidden, features = go.shape
    part = R // nx
    parts = 4
    hbm = pl.BlockSpec(memory_space=pltpu.HBM)
    vmem = pl.BlockSpec(memory_space=pltpu.VMEM)
    shape = jax.ShapeDtypeStruct
    uq, rq, uo, ro, gq, eq, go, eo = pl.pallas_call(
        functools.partial(exchange, ny, nc, nx, nz),
        out_shape=(
            shape((R, rows), F32), shape((R, columns), F32), shape((R, hidden), F32), shape((R, features), F32),
            shape((rows, columns), BF16), shape((rows, columns), BF16),
            shape((hidden, features), BF16), shape((hidden, features), BF16),
        ),
        in_specs=[hbm] * 6,
        out_specs=(vmem,) * 8,
        scratch_shapes=[
            pltpu.VMEM((R, columns), F32),
            pltpu.VMEM((R, features), F32),
            pltpu.SemaphoreType.DMA((6,)),
            pltpu.VMEM((2, nt, nx, part, LANES), F32),
            pltpu.VMEM((2, nt * nx - 1, part, LANES), F32),
            pltpu.VMEM((2, nz, part, LANES), F32),
            pltpu.VMEM((2, nt * nx, part, LANES), F32),
            pltpu.VMEM((2, nx, part, hidden), F32),
            pltpu.VMEM((2, nx - 1, part, hidden), F32),
            pltpu.VMEM((2, nz, part, hidden), F32),
            pltpu.VMEM((2, nx, part, hidden), F32),
            pltpu.VMEM((nt, 8, LANES), F32),
            pltpu.SemaphoreType.DMA((16,)),
            pltpu.SemaphoreType.DMA((16,)),
            pltpu.SemaphoreType.REGULAR,
        ],
        compiler_params=pltpu.CompilerParams(
            collective_id=0, has_side_effects=True, vmem_limit_bytes=24576 * 1024
        ),
    )(*(pltpu.with_memory_space_constraint(i, pltpu.HBM) for i in (gq, eq, basis_query.T, go, eo, basis_output.T)))
    outs = pl.pallas_call(
        functools.partial(finish, nx * nz, parts),
        out_shape=(
            shape((rows, columns), BF16), shape((hidden, features), BF16),
            shape((rows, columns), BF16), shape((hidden, features), BF16),
            shape((R, columns), F32), shape((R, features), F32),
        ),
        in_specs=[vmem] * 8,
        out_specs=(hbm,) * 6,
        scratch_shapes=[
            pltpu.VMEM((rows, columns), BF16),
            pltpu.VMEM((hidden, features), BF16),
            pltpu.VMEM((rows, columns), BF16),
            pltpu.VMEM((hidden, features), BF16),
            pltpu.SemaphoreType.DMA((2 + 4 * parts,)),
        ],
        compiler_params=pltpu.CompilerParams(vmem_limit_bytes=24 * 1024 * 1024),
    )(uq, rq, uo, ro, gq, eq, go, eo)
    return outs[0], outs[1], outs[2][None], outs[3][None], outs[4].T, outs[5].T


def solution(mesh):
    nt, n = mesh.shape["tensor"], mesh.shape["dp"]
    nx = 4 if n >= 64 else 2
    return jax.shard_map(
        functools.partial(local, (nt // 2, 2, nx, n // nx)),
        mesh=mesh,
        in_specs=(
            P("dp", None, "tensor"),
            P("dp", None, "tensor"),
            P("tensor", None),
            P("dp", "tensor", None),
            P("dp", "tensor", None),
            P(),
        ),
        out_specs=(
            P(None, "tensor"),
            P("tensor", None),
            P("dp", None, "tensor"),
            P("dp", "tensor", None),
            P("tensor", None),
            P(),
        ),
        check_vma=False,
    )
```
